256 devices in a mesh: rows: 64 (over x, z, core), sub: 4 (over y).
Axes of the slice: x: 4, y: 4, z: 8, core: 2. Of those that a mesh axis runs over, the one named last changes fastest.
Arguments:
- a_tiles: bfloat16 [2560, 8, 128, 128], P(('rows', 'sub')), may hold values from -0.1875 to 0.1875
- a_cols: int32 [2560, 8], P(('rows', 'sub')), may hold values from 0 to 2559, as said below
- a_count: int32 [2560], P(('rows', 'sub')), may hold values from 4 to 8, as said below
- p_tiles: bfloat16 [2560, 3, 128, 128], P(('rows', 'sub')), may hold values from -1 to 1
- aggregate: int32 [256, 10], replicated, may hold values from 0 to 4, never falling along the last dimension, each value on 1 to 3 neighbouring positions
- rep_list: int32 [256, 2, 4], replicated, may hold values from 0 to 9, as said below
Outputs:
- coarse: bfloat16 [1280, 21, 128, 128], P(('rows', 'sub'))
The draws below stay inside these ranges and needn't reach their ends.
Inputs may be any that keep to these rules, and one draw needn't show every extreme that they name: `a_cols`: each entry is a fine panel within 8 panels of its row panel; slot 0 is the row panel itself; the entries of a row panel are distinct; a panel of another device appears only if it is on that device's replication list toward this one. The live slots of a row panel are its first a_count slots; 8 is reached. `rep_list`: row 0 holds 4 distinct ascending indices among the device's first 8 panels, row 1 among its last 8. `aggregate`: along a device's panels never falling and rising by at most one; every coarse panel of a device has 1 to 3 fine panels, and 3 is reached.
All inputs are finite; a program needn't handle non-finite values.
Results may differ from the reference program's by a relative error of at most 0.0051.
Values may be sent and summed in bfloat16 or wider, within the bound.
A program may use at most 128 MiB of HBM per device.

```python
import math
import jax
import jax.numpy as jnp
import numpy as np
from jax import lax

PANEL = 128
KA = 8
REACH = 8
REP = 4
FP_DEV = 10
CP_DEV = 5
NFP = 2560
DEVICES = 256


def coupling_pattern(key):
    total = DEVICES * FP_DEV
    span = 2 * REACH + 1
    first, second, third = jax.random.split(key, 3)
    scores = jax.random.randint(first, (DEVICES, 2, REACH), 0, 65536) * REACH + jnp.arange(REACH, dtype=jnp.int32)
    _, picked = lax.top_k(scores, REP)
    picked = jnp.sort(picked.astype(jnp.int32), axis=-1)
    replicas = picked + jnp.array([0, FP_DEV - REACH], jnp.int32)[None, :, None]
    member = jnp.any(jnp.arange(FP_DEV, dtype=jnp.int32)[None, None, :, None] == replicas[:, :, None, :], axis=-1)
    member = jnp.transpose(member, (1, 0, 2)).reshape(2, total)
    rows = jnp.arange(total, dtype=jnp.int32)
    offsets = jnp.arange(span, dtype=jnp.int32) - REACH
    target = rows[:, None] + offsets[None, :]
    inside = (target >= 0) & (target < total)
    clipped = jnp.clip(target, 0, total - 1)
    own_dev = rows[:, None] // FP_DEV
    target_dev = clipped // FP_DEV
    upper = (target_dev == own_dev + 1) & member[0][clipped]
    lower = (target_dev == own_dev - 1) & member[1][clipped]
    usable = inside & ((target_dev == own_dev) | upper | lower)
    weights = jax.random.randint(second, (total, span), 0, 65536) * span + jnp.arange(span, dtype=jnp.int32)[None, :]
    weights = jnp.where(usable, weights, -1 - jnp.arange(span, dtype=jnp.int32)[None, :])
    weights = jnp.where(offsets[None, :] == 0, 1 << 30, weights)
    _, chosen = lax.top_k(weights, KA)
    columns = rows[:, None] + chosen.astype(jnp.int32) - REACH
    counts = jax.random.randint(third, (total,), KA // 2, KA + 1).astype(jnp.int32)
    counts = counts.at[0].set(KA)
    return (columns, counts, replicas)


def draw_a_cols(key, part):
    return coupling_pattern(key)[0]


def draw_a_count(key, part):
    return coupling_pattern(key)[1]


def draw_rep_list(key, part):
    return coupling_pattern(key)[2]


def block_levels(own_key, extent, shards, low, largest):
    gain = 1.0
    for axis_at, shards_of in shards:
        heights = jax.random.uniform(jax.random.fold_in(jax.random.fold_in(own_key, 6), axis_at), (shards_of,), jnp.float32, low / len(shards), largest / len(shards))
        gain = gain * jnp.repeat(jnp.exp(heights), extent[axis_at] // shards_of).reshape((-1,) + (1,) * (len(extent) - 1 - axis_at))
    return gain


def split_up(count, total, most, slope):
    loads = [(1 << 20) // math.isqrt(grade ** slope) + 1 for grade in range(2, count + 1)]
    surplus, given = total - most - (count - 1), [1] * (count - 1)
    while surplus > 0:
        movable = [i for i in range(count - 1) if given[i] < most]
        pool, left = sum([loads[i] for i in movable]), surplus
        for i in movable:
            extra = min(most - given[i], max(1, left * loads[i] // pool), surplus)
            given[i] = given[i] + extra
            surplus = surplus - extra
    return np.array([most] + given)


def uneven_parts(stream_key, amount, total, reach, lean):
    if amount == 2:
        one = jax.random.randint(stream_key, (), max(1, total - reach), min(reach, total - 1) + 1)
        return jnp.stack([one, total - one])
    tallies = jnp.asarray(split_up(amount, total, reach, lean), jnp.int32)
    pairs = (amount - 1) // 2
    donor, sink = tallies[1:1 + 2 * pairs:2], tallies[2:2 + 2 * pairs:2]
    slack = jnp.minimum(donor - 1, reach - sink)
    moved = jax.random.randint(jax.random.fold_in(stream_key, 1), (pairs,), 0, 1 << 20) % (slack + 1)
    tallies = tallies.at[1:1 + 2 * pairs:2].set(donor - moved).at[2:2 + 2 * pairs:2].set(sink + moved)
    return tallies[jax.random.permutation(jax.random.fold_in(stream_key, 2), amount)]


def noise(rng, dims, deviation, most, cuts=(), kind=jnp.bfloat16):
    gain = block_levels(rng, dims, cuts, -0.22, 0.18) if cuts else 1.0
    values = jax.random.normal(rng, dims, jnp.float32) * deviation * gain
    return jnp.minimum(jnp.maximum(values, -most), most).astype(kind)


def setup_inputs(seed: int = 0) -> dict:
    keys = jax.random.split(jax.random.key(seed), 7)
    a_tiles = noise(keys[0], (NFP, KA, PANEL, PANEL), (KA * PANEL) ** -0.5, 0.1875, ((0, 256),))
    a_cols = draw_a_cols(jax.random.fold_in(keys[6], 71), 0)
    a_count = draw_a_count(jax.random.fold_in(keys[6], 71), 0)
    p_tiles = noise(keys[3], (NFP, 3, PANEL, PANEL), (PANEL // 4) ** -0.5, 1.0, ((0, 256),))
    aggregate = jax.vmap(lambda own: jnp.searchsorted(jnp.cumsum(uneven_parts(own, CP_DEV, FP_DEV, 3, 1)), jnp.arange(FP_DEV), side="right"))(jax.random.split(keys[4], DEVICES)).reshape((DEVICES, FP_DEV)).astype(jnp.int32)
    rep_list = draw_rep_list(jax.random.fold_in(keys[6], 71), 0)
    return dict(a_tiles=a_tiles, a_cols=a_cols, a_count=a_count, p_tiles=p_tiles, aggregate=aggregate, rep_list=rep_list)


def coarse_rows(dev, a_blk, cols, count, p_ext, aggregate, rep_list):
    fp = a_blk.shape[0]
    ka = a_blk.shape[1]
    pb = a_blk.shape[2]
    ndev = aggregate.shape[0]
    total = ndev * fp
    ncoarse = ndev * CP_DEV
    kw = 2 * REACH + 3
    kc = 2 * REACH + 5
    flat = aggregate.reshape(-1)
    base = dev * fp

    def coarse_of(index):
        held = jnp.clip(index, 0, total - 1)
        return (held // fp) * CP_DEV + flat[held]

    g_own = coarse_of(base + jnp.arange(fp, dtype=jnp.int32))
    g_col = coarse_of(cols)
    dev_col = jnp.clip(cols, 0, total - 1) // fp
    local_col = cols % fp
    side = jnp.where(dev_col > dev, 0, 1)
    listed = jnp.any(rep_list[dev_col, side, :] == local_col[:, :, None], axis=-1)
    live = (jnp.arange(ka, dtype=jnp.int32)[None, :] < count[:, None]) & ((dev_col == dev) | listed)
    shifts = jnp.arange(3, dtype=jnp.int32) - 1
    own_target = g_own[:, None] + shifts[None, :]
    own_live = (own_target >= 0) & (own_target < ncoarse)
    col_target = g_col[:, :, None] + shifts[None, None, :]
    col_live = (col_target >= 0) & (col_target < ncoarse)
    slot_base = (g_col - g_own[:, None] + REACH).astype(jnp.int32)
    lead = g_own - dev * CP_DEV
    ext_index = cols - base + REACH
    a_use = a_blk * live[:, :, None, None].astype(jnp.bfloat16)
    p_own = p_ext[REACH:REACH + fp] * own_live[:, :, None, None].astype(jnp.bfloat16)

    def step(panel, acc):
        picked = jnp.take(p_ext, ext_index[panel], axis=0)
        picked = picked * col_live[panel][:, :, None, None].astype(jnp.bfloat16)
        prods = jnp.einsum('kab,kqbc->kqac', a_use[panel].astype(jnp.float32), picked.astype(jnp.float32))
        window = jnp.zeros((kw, pb, pb), jnp.float32)
        for slot_k in range(ka):
            where = slot_base[panel, slot_k]
            current = lax.dynamic_slice_in_dim(window, where, 3, 0)
            window = lax.dynamic_update_slice_in_dim(window, current + prods[slot_k], where, 0)
        product = window.astype(jnp.bfloat16)
        for block in range(3):
            term = jnp.einsum('ba,rbc->rac', p_own[panel, block].astype(jnp.float32), product.astype(jnp.float32))
            term = jnp.pad(term, ((2 - block, block), (0, 0), (0, 0)))
            row = lead[panel] + block
            current = lax.dynamic_slice_in_dim(acc, row, 1, 0)
            acc = lax.dynamic_update_slice_in_dim(acc, current + term[None], row, 0)
        return acc

    start = jnp.zeros((CP_DEV + 2, kc, pb, pb), jnp.float32)
    return lax.fori_loop(0, fp, step, start)


def reference(a_tiles, a_cols, a_count, p_tiles, aggregate, rep_list):
    ndev = aggregate.shape[0]
    fp = FP_DEV
    kc = 2 * REACH + 5
    pb = a_tiles.shape[2]
    p_pad = jnp.pad(p_tiles, ((REACH, REACH), (0, 0), (0, 0), (0, 0)))

    def one_device(carry, dev):
        pending, ghost_prev = carry
        first = dev * fp
        a_blk = lax.dynamic_slice_in_dim(a_tiles, first, fp, 0)
        cols = lax.dynamic_slice_in_dim(a_cols, first, fp, 0)
        count = lax.dynamic_slice_in_dim(a_count, first, fp, 0)
        p_ext = lax.dynamic_slice_in_dim(p_pad, first, fp + 2 * REACH, 0)
        acc = coarse_rows(dev, a_blk, cols, count, p_ext, aggregate, rep_list)
        lower_ghost = acc[0].astype(jnp.bfloat16).astype(jnp.float32)
        upper_ghost = acc[CP_DEV + 1].astype(jnp.bfloat16)
        emitted = pending.at[CP_DEV - 1].add(lower_ghost).astype(jnp.bfloat16)
        own = acc[1:CP_DEV + 1]
        own = own.at[0].add(ghost_prev.astype(jnp.float32))
        return (own, upper_ghost), emitted

    start = (jnp.zeros((CP_DEV, kc, pb, pb), jnp.float32), jnp.zeros((kc, pb, pb), jnp.bfloat16))
    final, emitted = lax.scan(one_device, start, jnp.arange(ndev, dtype=jnp.int32))
    last = final[0].astype(jnp.bfloat16)
    blocks = jnp.concatenate([emitted[1:], last[None]], axis=0)
    return blocks.reshape(ndev * CP_DEV, kc, pb, pb)
```

```python
import functools

import jax
import jax.numpy as jnp
from jax import lax
from jax.experimental import pallas as pl
from jax.experimental.pallas import tpu as pltpu
from jax.sharding import PartitionSpec as P

B = 128
FP = 10
CP = 5
KA = 8
REP = 4
NJ = FP + 2 * REP
NT = 17
T0 = -6
KC = 21
MESH = pl.DeviceIdType.MESH


def blk(n, count=1):
    return pl.ds(n * B, count * B)


def dot(x, y):
    return jnp.dot(x, y, preferred_element_type=jnp.float32)


def kernel(
    ndev, nsub,
    cols_s, cnt_s, agg_h, rep_h, a_h, p_h,
    out,
    agg_s, rep_s, p_v, pt_v, a_v, ad, r, ra, pd, pl_own, acc,
    sendp, recvp, sendg, recvg, sendc, recvc,
    meta_sem, load_sem, send_sem, recv_sem,
):
    e = lax.axis_index("rows") * nsub + lax.axis_index("sub")
    up = lax.rem(e + 1, ndev)
    dn = lax.rem(e + ndev - 1, ndev)
    peers = ((dn // nsub, lax.rem(dn, nsub)), (up // nsub, lax.rem(up, nsub)))

    barrier = pltpu.get_barrier_semaphore()
    for peer in peers:
        pl.semaphore_signal(barrier, inc=1, device_id=peer, device_id_type=MESH)

    load_p = pltpu.make_async_copy(p_h, p_v.at[pl.ds(0, 3 * FP)], load_sem.at[0])
    load_p.start()
    meta = []
    for n, d in enumerate((dn, e, up)):
        meta.append(pltpu.make_async_copy(agg_h.at[d], agg_s.at[n], meta_sem.at[n]))
        meta.append(pltpu.make_async_copy(rep_h.at[d], rep_s.at[n], meta_sem.at[3 + n]))
    for copy in meta:
        copy.start()
    load_a = pltpu.make_async_copy(a_h, a_v.at[pl.ds(0, KA * FP)], load_sem.at[1])
    load_a.start()

    zero = jnp.zeros((B, B), jnp.bfloat16)
    p_v[3 * FP] = zero
    pt_v[3 * FP] = zero
    a_v[KA * FP] = zero
    recvp[0, 3 * REP] = zero
    recvp[1, 3 * REP] = zero

    for copy in meta:
        copy.wait()
    load_p.wait()

    def agg(i):
        return agg_s[1, 0, i]

    for i in range(3):
        low = jnp.where((e == 0) & (agg(i) == 0), 3 * FP, 3 * i)
        p_v[3 * i] = p_v[low]
        k = FP - 1 - i
        high = jnp.where((e == ndev - 1) & (agg(k) == CP - 1), 3 * FP, 3 * k + 2)
        p_v[3 * k + 2] = p_v[high]

    for d in range(2):
        for s in range(REP):
            local = rep_s[1, d, s]
            for q in range(3):
                sendp[d, 3 * s + q] = p_v[3 * local + q]

    def remote(d, n, src, dst):
        return pltpu.make_async_remote_copy(
            src_ref=src, dst_ref=dst, send_sem=send_sem.at[d, n], recv_sem=recv_sem.at[d, n],
            device_id=peers[d], device_id_type=MESH,
        )

    send_p = [remote(d, 0, sendp.at[d], recvp.at[d, pl.ds(0, 3 * REP)]) for d in range(2)]
    send_g = [remote(d, 1, sendg.at[d], recvg.at[d]) for d in range(2)]
    send_c = [remote(d, 2, sendc.at[d], recvc.at[d]) for d in range(2)]
    pl.semaphore_wait(barrier, 2)
    for copy in send_p:
        copy.start()

    def transpose(b, carry):
        pt_v[b] = p_v[b].T
        return carry

    lax.fori_loop(0, 3 * FP, transpose, 0)

    def pick(q, first, none):
        return jnp.where((q >= 0) & (q <= 2), first + q, none)

    for i in range(FP):
        for c in range(CP + 2):
            if (c == 0 and i > 2) or (c == CP + 1 and i < FP - 3):
                continue
            r[blk(c), blk(i)] = pt_v[pick(c - agg(i), 3 * i, 3 * FP)]

    ids = []
    for s in range(REP):
        ids.append(rep_s[0, 1, s] - FP)
    for j in range(FP):
        ids.append(j)
    for s in range(REP):
        ids.append(rep_s[2, 0, s] + FP)

    load_a.wait()

    def spread(i, carry):
        held = [jnp.where(k < cnt_s[i], cols_s[i, k] - e * FP, 1 << 20) for k in range(KA)]
        rows = pl.ds(pl.multiple_of(i * B, B), B)
        for j in range(NJ):
            at = KA * FP
            for k in range(KA):
                at = jnp.where(held[k] == ids[j], i * KA + k, at)
            ad[rows, blk(j)] = a_v[at]
        return carry

    lax.fori_loop(0, FP, spread, 0)

    for c, i in ((0, 0), (CP + 1, FP - 3)):
        for n in range(0, NJ, 6):
            ra[blk(c), blk(n, 6)] = dot(r[blk(c), blk(i, 3)], ad[blk(i, 3), blk(n, 6)]).astype(jnp.bfloat16)

    for j in range(FP):
        for t in range(-1, CP + 1):
            pd[blk(REP + j), blk(t - T0)] = p_v[pick(t - agg(j) + 1, 3 * j, 3 * FP)]

    own = blk(REP, FP)
    for d, c, first, t in ((0, 0, 0, -1), (1, CP + 1, REP + FP, 1)):
        for s in range(REP):
            sendg[d, s] = ra[blk(c), blk(first + s)]
        part = dot(ra[blk(c), own], pd[own, blk(t - T0, 5)]).astype(jnp.bfloat16)
        for n in range(5):
            sendg[d, REP + n] = part[:, n * B : (n + 1) * B]

    mid = blk(1, CP)

    def left(n, carry):
        at = pl.ds(pl.multiple_of(n * 2 * B, 2 * B), 2 * B)
        ra[mid, at] = dot(r[mid, :], ad[:, at]).astype(jnp.bfloat16)
        return carry

    lax.fori_loop(0, NJ // 2, left, 0)

    for d in range(2):
        for s in range(REP):
            local = rep_s[1, d, s]
            for t in range(-1, CP + 1):
                pl_own[d, blk(s), blk(t + 1)] = p_v[pick(t - agg(local) + 1, 3 * local, 3 * FP)]

    def emit(t, count, first, panels):
        part = dot(ra[mid, blk(first, panels)], pd[blk(first, panels), blk(t - T0, count)])
        for n in range(count):
            for c in range(CP):
                block = part[c * B : (c + 1) * B, n * B : (n + 1) * B]
                if c in (0, CP - 1):
                    acc[0 if c == 0 else 1, :, blk(t + n - T0)] = block
                else:
                    out[c, t + n - c + 10] = block.astype(jnp.bfloat16)

    emit(1, 3, REP, FP)

    for copy in send_p:
        copy.wait()
    for copy in send_g:
        copy.start()

    for s in range(REP):
        g = agg_s[0, 0, rep_s[0, 1, s]] - CP
        for t in range(-6, 1):
            pd[blk(s), blk(t - T0)] = recvp[1, pick(t - g + 1, 3 * s, 3 * REP)]
        g = agg_s[2, 0, rep_s[2, 0, s]] + CP
        for t in range(4, 11):
            pd[blk(REP + FP + s), blk(t - T0)] = recvp[0, pick(t - g + 1, 3 * s, 3 * REP)]

    last = REP + FP
    part = dot(ra[blk(0), blk(REP, FP + 1)], pd[blk(REP, FP + 1), blk(4 - T0, 2)]).astype(jnp.bfloat16)
    sendc[0, 0] = part[:, :B]
    sendc[0, 1] = part[:, B:]
    sendc[0, 2] = dot(ra[blk(0), blk(last)], pd[blk(last), blk(6 - T0)]).astype(jnp.bfloat16)
    part = dot(ra[blk(CP + 1), blk(REP - 1, FP + 1)], pd[blk(REP - 1, FP + 1), blk(-1 - T0, 2)]).astype(jnp.bfloat16)
    sendc[1, 1] = part[:, :B]
    sendc[1, 2] = part[:, B:]
    sendc[1, 0] = dot(ra[blk(CP + 1), blk(REP - 1)], pd[blk(REP - 1), blk(-2 - T0)]).astype(jnp.bfloat16)
    for copy in send_c:
        copy.start()

    emit(-1, 2, 0, REP + FP)
    emit(4, 2, REP, FP + REP)
    emit(-6, 5, 0, REP)
    emit(6, 5, REP + FP, REP)

    for c in range(CP):
        for m in range(KC):
            low, high = (3 if c == 0 else CP - 1 - c), (17 if c == CP - 1 else KC - 1 - c)
            if not low <= m <= high:
                out[c, m] = zero

    for copy in send_g:
        copy.wait()
    for copy in send_c:
        copy.wait()

    for d, c, n in ((1, 0, 0), (0, CP - 1, 1)):
        factor = jnp.concatenate([recvg[d, s] for s in range(REP)], axis=1)
        extra = dot(factor, pl_own[n])
        for t in range(T0 - 1, T0 + NT + 1):
            m = t - c + 10
            if not 0 <= m < KC:
                continue
            terms = []
            if T0 <= t < T0 + NT:
                terms.append(acc[n, :, blk(t - T0)])
            if -1 <= t <= CP:
                terms.append(extra[:, (t + 1) * B : (t + 2) * B])
            sent = t + CP if d == 1 else t - CP
            early, late = (1, -2) if d == 1 else (-1, 4)
            if early <= sent < early + 5:
                terms.append(recvg[d, REP + sent - early].astype(jnp.float32))
            if late <= sent < late + 3:
                terms.append(recvc[d, sent - late].astype(jnp.float32))
            if terms:
                out[c, m] = functools.reduce(jnp.add, terms).astype(jnp.bfloat16)


def body(ndev, nsub, a_tiles, a_cols, a_count, p_tiles, aggregate, rep_list):
    bf16 = jnp.bfloat16
    vmem = pltpu.VMEM
    return pl.pallas_call(
        functools.partial(kernel, ndev, nsub),
        out_shape=jax.ShapeDtypeStruct((CP, KC, B, B), bf16),
        in_specs=[pl.BlockSpec(memory_space=pltpu.SMEM)] * 2 + [pl.BlockSpec(memory_space=pl.ANY)] * 4,
        out_specs=pl.BlockSpec(memory_space=pltpu.VMEM),
        scratch_shapes=[
            pltpu.SMEM((3, 1, FP), jnp.int32),
            pltpu.SMEM((3, 2, REP), jnp.int32),
            vmem((3 * FP + 1, B, B), bf16),
            vmem((3 * FP + 1, B, B), bf16),
            vmem((KA * FP + 1, B, B), bf16),
            vmem((FP * B, NJ * B), bf16),
            vmem(((CP + 2) * B, FP * B), bf16),
            vmem(((CP + 2) * B, NJ * B), bf16),
            vmem((NJ * B, NT * B), bf16),
            vmem((2, REP * B, 7 * B), bf16),
            vmem((2, B, NT * B), jnp.float32),
            vmem((2, 3 * REP, B, B), bf16),
            vmem((2, 3 * REP + 1, B, B), bf16),
            vmem((2, REP + 5, B, B), bf16),
            vmem((2, REP + 5, B, B), bf16),
            vmem((2, 3, B, B), bf16),
            vmem((2, 3, B, B), bf16),
            pltpu.SemaphoreType.DMA((6,)),
            pltpu.SemaphoreType.DMA((2,)),
            pltpu.SemaphoreType.DMA((2, 3)),
            pltpu.SemaphoreType.DMA((2, 3)),
        ],
        compiler_params=pltpu.CompilerParams(
            collective_id=0, has_side_effects=True, vmem_limit_bytes=56 << 20
        ),
        name="coarse",
    )(
        a_cols,
        a_count,
        aggregate.reshape(ndev, 1, FP),
        rep_list,
        a_tiles.reshape(FP * KA, B, B),
        p_tiles.reshape(FP * 3, B, B),
    )


def solution(mesh):
    in_specs = (
        P(("rows", "sub"), None, None, None),
        P(("rows", "sub"), None),
        P(("rows", "sub")),
        P(("rows", "sub"), None, None, None),
        P(),
        P(),
    )
    out_specs = P(("rows", "sub"), None, None, None)
    run = functools.partial(body, mesh.size, mesh.shape["sub"])
    return jax.shard_map(run, mesh=mesh, in_specs=in_specs, out_specs=out_specs, check_vma=False)
```

```python
import functools

import jax
import jax.numpy as jnp
from jax import lax
from jax.experimental import pallas as pl
from jax.experimental.pallas import tpu as pltpu
from jax.sharding import PartitionSpec as P

B = 128
FP = 10
CP = 5
KA = 8
REP = 4
NJ = FP + 2 * REP
NT = 17
T0 = -6
KC = 21
MESH = pl.DeviceIdType.MESH


def blk(n, count=1):
    return pl.ds(n * B, count * B)


def dot(x, y):
    return jnp.dot(x, y, preferred_element_type=jnp.float32)


def kernel(
    ndev, nsub,
    cols_h, cnt_h, agg_h, rep_h, a_h, p_h,
    out,
    cols_s, cnt_s, agg_s, rep_s, p_v, pt_v, a_v, ad, r, ra, pd, pl_own, acc,
    sendp, recvp_up, recvp_dn, sendg, recvg, sendc, recvc,
    load_sem, send_sem, recv_sem, ready_sem,
):
    e = lax.axis_index("rows") * nsub + lax.axis_index("sub")
    up = lax.rem(e + 1, ndev)
    dn = lax.rem(e + ndev - 1, ndev)
    peers = ((dn // nsub, lax.rem(dn, nsub)), (up // nsub, lax.rem(up, nsub)))

    has_dn = e > 0
    has_up = e < ndev - 1
    sends, receives = (has_dn, has_up), (has_up, has_dn)

    barrier = pltpu.get_barrier_semaphore()

    @pl.when(has_dn)
    def _():
        pl.semaphore_signal(barrier, inc=1, device_id=peers[0], device_id_type=MESH)

    load_p = pltpu.make_async_copy(p_h, p_v.at[pl.ds(0, 3 * FP)], load_sem.at[0])
    load_p.start()
    meta = [
        pltpu.make_async_copy(src, dst, load_sem.at[2 + n])
        for n, (src, dst) in enumerate(((rep_h, rep_s), (agg_h, agg_s), (cols_h, cols_s), (cnt_h, cnt_s)))
    ]
    for copy in meta:
        copy.start()
    load_a = pltpu.make_async_copy(a_h, a_v.at[pl.ds(0, KA * FP)], load_sem.at[1])
    load_a.start()

    recvp = (recvp_up, recvp_dn)

    zero = jnp.zeros((B, B), jnp.bfloat16)
    p_v[3 * FP] = zero
    pt_v[3 * FP] = zero
    a_v[KA * FP] = zero
    recvp_up[3 * REP] = zero
    recvp_dn[3 * REP] = zero


    @pl.when(has_up)
    def _():
        pl.semaphore_wait(barrier, 1)
        pl.semaphore_signal(ready_sem, inc=1, device_id=peers[1], device_id_type=MESH)

    for copy in meta:
        copy.wait()
    load_p.wait()

    def agg(i):
        return agg_s[i, e]

    for i in range(3):
        low = jnp.where((e == 0) & (agg(i) == 0), 3 * FP, 3 * i)
        p_v[3 * i] = p_v[low]
        k = FP - 1 - i
        high = jnp.where((e == ndev - 1) & (agg(k) == CP - 1), 3 * FP, 3 * k + 2)
        p_v[3 * k + 2] = p_v[high]

    def remote(d, n, src, dst):
        return pltpu.make_async_remote_copy(
            src_ref=src, dst_ref=dst, send_sem=send_sem.at[d, n], recv_sem=recv_sem.at[d, n],
            device_id=peers[d], device_id_type=MESH,
        )

    send_p = [remote(d, 0, sendp.at[d], recvp[d].at[pl.ds(0, 3 * REP)]) for d in range(2)]
    send_g = [remote(d, 1, sendg.at[d], recvg.at[d]) for d in range(2)]
    send_c = [remote(d, 2, sendc.at[d], recvc.at[d]) for d in range(2)]

    def start(copies, d):
        pl.when(sends[d])(copies[d].start)

    def arrived(copies, d):
        pl.when(receives[d])(copies[d].wait_recv)

    for d in (1, 0):
        for s in range(REP):
            local = rep_s[d, s, e]
            for q in range(3):
                sendp[d, 3 * s + q] = p_v[3 * local + q]
        if d == 0:
            pl.when(has_dn)(lambda: pl.semaphore_wait(ready_sem, 1))
        start(send_p, d)

    for d in range(2):
        @pl.when(jnp.logical_not(receives[d]))
        def _():
            recvp[d][...] = jnp.zeros(recvp[d].shape, jnp.bfloat16)
            recvg[d] = jnp.zeros(recvg.shape[1:], jnp.bfloat16)
            recvc[d] = jnp.zeros(recvc.shape[1:], jnp.bfloat16)

    def transpose(b, carry):
        pt_v[b] = p_v[b].T
        return carry

    lax.fori_loop(0, 3 * FP, transpose, 0)

    def pick(q, first, none):
        return jnp.where((q >= 0) & (q <= 2), first + q, none)

    for i in range(FP):
        for c in range(CP + 2):
            if (c == 0 and i > 2) or (c == CP + 1 and i < FP - 3):
                continue
            r[blk(c), blk(i)] = pt_v[pick(c - agg(i), 3 * i, 3 * FP)]

    ids = []
    for s in range(REP):
        ids.append(rep_s[1, s, dn] - FP)
    for j in range(FP):
        ids.append(j)
    for s in range(REP):
        ids.append(rep_s[0, s, up] + FP)

    load_a.wait()

    def spread(i, carry):
        held = [jnp.where(k < cnt_s[0, i], cols_s[k, i] - e * FP, 1 << 20) for k in range(KA)]
        rows = pl.ds(pl.multiple_of(i * B, B), B)
        for j in range(NJ):
            at = KA * FP
            for k in range(KA):
                at = jnp.where(held[k] == ids[j], i * KA + k, at)
            ad[rows, blk(j)] = a_v[at]
        return carry

    lax.fori_loop(0, FP, spread, 0)

    for c, i in ((0, 0), (CP + 1, FP - 3)):
        for n in range(0, NJ, 6):
            ra[blk(c), blk(n, 6)] = dot(r[blk(c), blk(i, 3)], ad[blk(i, 3), blk(n, 6)]).astype(jnp.bfloat16)

    for j in range(FP):
        for t in range(-1, CP + 1):
            pd[blk(REP + j), blk(t - T0)] = p_v[pick(t - agg(j) + 1, 3 * j, 3 * FP)]

    own = blk(REP, FP)
    for d, c, first, t in ((0, 0, 0, -1), (1, CP + 1, REP + FP, 1)):
        for s in range(REP):
            sendg[d, s] = ra[blk(c), blk(first + s)]
        part = dot(ra[blk(c), own], pd[own, blk(t - T0, 5)]).astype(jnp.bfloat16)
        for n in range(5):
            sendg[d, REP + n] = part[:, n * B : (n + 1) * B]

    for d in (1, 0):
        start(send_g, d)

    mid = blk(1, CP)

    def left(n, carry):
        at = pl.ds(pl.multiple_of(n * 2 * B, 2 * B), 2 * B)
        ra[mid, at] = dot(r[mid, :], ad[:, at]).astype(jnp.bfloat16)
        return carry

    lax.fori_loop(0, NJ // 2, left, 0)

    for d in range(2):
        for s in range(REP):
            local = rep_s[d, s, e]
            for t in range(-1, CP + 1):
                pl_own[d, blk(s), blk(t + 1)] = p_v[pick(t - agg(local) + 1, 3 * local, 3 * FP)]

    def emit(t, count, first, panels):
        part = dot(ra[mid, blk(first, panels)], pd[blk(first, panels), blk(t - T0, count)])
        for n in range(count):
            for c in range(CP):
                block = part[c * B : (c + 1) * B, n * B : (n + 1) * B]
                if c in (0, CP - 1):
                    acc[0 if c == 0 else 1, :, blk(t + n - T0)] = block
                else:
                    out[c, t + n - c + 10] = block.astype(jnp.bfloat16)

    emit(1, 3, REP, FP)

    last = REP + FP
    arrived(send_p, 0)
    for s in range(REP):
        g = agg_s[rep_s[0, s, up], up] + CP
        for t in range(4, 11):
            pd[blk(last + s), blk(t - T0)] = recvp_up[pick(t - g + 1, 3 * s, 3 * REP)]
    part = dot(ra[blk(0), blk(REP, FP + 1)], pd[blk(REP, FP + 1), blk(4 - T0, 2)]).astype(jnp.bfloat16)
    sendc[0, 0] = part[:, :B]
    sendc[0, 1] = part[:, B:]
    sendc[0, 2] = dot(ra[blk(0), blk(last)], pd[blk(last), blk(6 - T0)]).astype(jnp.bfloat16)
    start(send_c, 0)

    arrived(send_p, 1)
    for s in range(REP):
        g = agg_s[rep_s[1, s, dn], dn] - CP
        for t in range(-6, 1):
            pd[blk(s), blk(t - T0)] = recvp_dn[pick(t - g + 1, 3 * s, 3 * REP)]
    part = dot(ra[blk(CP + 1), blk(REP - 1, FP + 1)], pd[blk(REP - 1, FP + 1), blk(-1 - T0, 2)]).astype(jnp.bfloat16)
    sendc[1, 1] = part[:, :B]
    sendc[1, 2] = part[:, B:]
    sendc[1, 0] = dot(ra[blk(CP + 1), blk(REP - 1)], pd[blk(REP - 1), blk(-2 - T0)]).astype(jnp.bfloat16)
    start(send_c, 1)

    emit(4, 2, REP, FP + REP)
    emit(6, 5, last, REP)
    emit(-1, 2, 0, REP + FP)
    emit(-6, 5, 0, REP)

    for c in range(CP):
        for m in range(KC):
            low, high = (3 if c == 0 else CP - 1 - c), (17 if c == CP - 1 else KC - 1 - c)
            if not low <= m <= high:
                out[c, m] = zero

    for d, c, n in ((0, CP - 1, 1), (1, 0, 0)):
        arrived(send_g, d)
        factor = jnp.concatenate([recvg[d, s] for s in range(REP)], axis=1)
        extra = dot(factor, pl_own[n])
        early, late = (1, -2) if d == 1 else (-1, 4)
        held = {}
        for t in range(T0 - 1, T0 + NT + 1):
            m = t - c + 10
            if not 0 <= m < KC:
                continue
            terms = []
            if T0 <= t < T0 + NT:
                terms.append(acc[n, :, blk(t - T0)])
            if -1 <= t <= CP:
                terms.append(extra[:, (t + 1) * B : (t + 2) * B])
            sent = t + CP if d == 1 else t - CP
            if early <= sent < early + 5:
                terms.append(recvg[d, REP + sent - early].astype(jnp.float32))
            total = functools.reduce(jnp.add, terms) if terms else None
            if late <= sent < late + 3:
                if total is not None:
                    acc[n, :, blk(t - T0)] = total
                held[m] = (sent - late, t, total is not None)
            elif terms:
                out[c, m] = total.astype(jnp.bfloat16)
        arrived(send_c, d)
        for m, (at, t, more) in held.items():
            total = recvc[d, at].astype(jnp.float32)
            if more:
                total = total + acc[n, :, blk(t - T0)]
            out[c, m] = total.astype(jnp.bfloat16)

    for copies in (send_p, send_g, send_c):
        for d in range(2):
            pl.when(sends[d])(copies[d].wait_send)


def body(ndev, nsub, a_tiles, a_cols, a_count, p_tiles, aggregate, rep_list):
    bf16 = jnp.bfloat16
    vmem = pltpu.VMEM
    return pl.pallas_call(
        functools.partial(kernel, ndev, nsub),
        out_shape=pltpu.VMEM((CP, KC, B, B), bf16),
        in_specs=[pl.BlockSpec(memory_space=pl.ANY)] * 6,
        out_specs=pl.BlockSpec(memory_space=pltpu.VMEM),
        scratch_shapes=[
            pltpu.SMEM((KA, FP), jnp.int32),
            pltpu.SMEM((1, FP), jnp.int32),
            pltpu.SMEM((FP, ndev), jnp.int32),
            pltpu.SMEM((2, REP, ndev), jnp.int32),
            vmem((3 * FP + 1, B, B), bf16),
            vmem((3 * FP + 1, B, B), bf16),
            vmem((KA * FP + 1, B, B), bf16),
            vmem((FP * B, NJ * B), bf16),
            vmem(((CP + 2) * B, FP * B), bf16),
            vmem(((CP + 2) * B, NJ * B), bf16),
            vmem((NJ * B, NT * B), bf16),
            vmem((2, REP * B, 7 * B), bf16),
            vmem((2, B, NT * B), jnp.float32),
            vmem((2, 3 * REP, B, B), bf16),
            vmem((3 * REP + 1, B, B), bf16),
            vmem((3 * REP + 1, B, B), bf16),
            vmem((2, REP + 5, B, B), bf16),
            vmem((2, REP + 5, B, B), bf16),
            vmem((2, 3, B, B), bf16),
            vmem((2, 3, B, B), bf16),
            pltpu.SemaphoreType.DMA((6,)),
            pltpu.SemaphoreType.DMA((2, 3)),
            pltpu.SemaphoreType.DMA((2, 3)),
            pltpu.SemaphoreType.REGULAR,
        ],
        compiler_params=pltpu.CompilerParams(
            collective_id=0, has_side_effects=True, vmem_limit_bytes=56 << 20
        ),
        name="coarse",
    )(
        a_cols.T,
        a_count.reshape(1, FP),
        aggregate.T,
        rep_list.transpose(1, 2, 0),
        a_tiles.reshape(FP * KA, B, B),
        p_tiles.reshape(FP * 3, B, B),
    )


def solution(mesh):
    in_specs = (
        P(("rows", "sub"), None, None, None),
        P(("rows", "sub"), None),
        P(("rows", "sub")),
        P(("rows", "sub"), None, None, None),
        P(),
        P(),
    )
    out_specs = P(("rows", "sub"), None, None, None)
    run = functools.partial(body, mesh.size, mesh.shape["sub"])
    return jax.shard_map(run, mesh=mesh, in_specs=in_specs, out_specs=out_specs, check_vma=False)
```

```python
import functools

import jax
import jax.numpy as jnp
from jax import lax
from jax.experimental import pallas as pl
from jax.experimental.pallas import tpu as pltpu
from jax.sharding import PartitionSpec as P

B = 128
FP = 10
CP = 5
KA = 8
REP = 4
NJ = FP + 2 * REP
NT = 17
T0 = -6
ROWS_X = 16
KC = 21
MESH = pl.DeviceIdType.MESH


def blk(n, count=1):
    return pl.ds(n * B, count * B)


def dot(x, y):
    return jnp.dot(x, y, preferred_element_type=jnp.float32)


def kernel(
    ndev, nsub,
    cols_h, cnt_h, agg_h, rep_h, a_h, p_h,
    out,
    cols_s, cnt_s, agg_s, rep_s, p_v, pt_v, a_v, ad, r, ra, pd, pl_own, acc,
    sendp, recvp_up, recvp_dn, sendg, recvg, sendc, recvc,
    load_sem, send_sem, recv_sem, ready_sem,
):
    e = lax.axis_index("rows") * nsub + lax.axis_index("sub")
    up = lax.rem(e + 1, ndev)
    dn = lax.rem(e + ndev - 1, ndev)
    peers = ((dn // nsub, lax.rem(dn, nsub)), (up // nsub, lax.rem(up, nsub)))

    has_dn = e > 0
    has_up = e < ndev - 1
    sends, receives = (has_dn, has_up), (has_up, has_dn)

    barrier = pltpu.get_barrier_semaphore()

    @pl.when(has_dn)
    def _():
        pl.semaphore_signal(barrier, inc=1, device_id=peers[0], device_id_type=MESH)

    load_p = pltpu.make_async_copy(p_h, p_v.at[pl.ds(0, 3 * FP)], load_sem.at[0])
    load_p.start()
    meta = [
        pltpu.make_async_copy(src, dst, load_sem.at[2 + n])
        for n, (src, dst) in enumerate(((rep_h, rep_s), (agg_h, agg_s), (cols_h, cols_s), (cnt_h, cnt_s)))
    ]
    for copy in meta:
        copy.start()
    load_a = pltpu.make_async_copy(a_h, a_v.at[pl.ds(0, KA * FP)], load_sem.at[1])

    recvp = (recvp_up, recvp_dn)

    load_a.start()
    zero = jnp.zeros((B, B), jnp.bfloat16)
    p_v[3 * FP] = zero
    pt_v[3 * FP] = zero
    a_v[KA * FP] = zero
    recvp_up[3 * REP] = zero
    recvp_dn[3 * REP] = zero


    @pl.when(has_up)
    def _():
        pl.semaphore_wait(barrier, 1)
        pl.semaphore_signal(ready_sem, inc=1, device_id=peers[1], device_id_type=MESH)

    for copy in meta:
        copy.wait()
    load_p.wait()

    def agg(i):
        return agg_s[i, e]

    for i in range(3):
        low = jnp.where((e == 0) & (agg(i) == 0), 3 * FP, 3 * i)
        p_v[3 * i] = p_v[low]
        k = FP - 1 - i
        high = jnp.where((e == ndev - 1) & (agg(k) == CP - 1), 3 * FP, 3 * k + 2)
        p_v[3 * k + 2] = p_v[high]

    def remote(d, n, src, dst):
        return pltpu.make_async_remote_copy(
            src_ref=src, dst_ref=dst, send_sem=send_sem.at[d, n], recv_sem=recv_sem.at[d, n],
            device_id=peers[d], device_id_type=MESH,
        )

    send_p = [remote(d, 0, sendp.at[d], recvp[d].at[pl.ds(0, 3 * REP)]) for d in range(2)]
    send_g = [remote(d, 1, sendg.at[d], recvg.at[d]) for d in range(2)]
    send_c = [remote(d, 2, sendc.at[d], recvc.at[d]) for d in range(2)]

    def start(copies, d):
        pl.when(sends[d])(copies[d].start)

    def arrived(copies, d):
        pl.when(receives[d])(copies[d].wait_recv)

    for d in (1, 0):
        for s in range(REP):
            local = rep_s[d, s, e]
            for q in range(3):
                sendp[d, 3 * s + q] = p_v[3 * local + q]
        if d == 1:
            start(send_p, d)

    def start_down():
        pl.semaphore_wait(ready_sem, 1)
        send_p[0].start()

    ahead = lax.rem(e, nsub * ROWS_X) == 0
    pl.when(has_dn & jnp.logical_not(ahead))(start_down)

    for d in range(2):
        @pl.when(jnp.logical_not(receives[d]))
        def _():
            recvp[d][...] = jnp.zeros(recvp[d].shape, jnp.bfloat16)
            recvg[d] = jnp.zeros(recvg.shape[1:], jnp.bfloat16)
            recvc[d] = jnp.zeros(recvc.shape[1:], jnp.bfloat16)

    def transpose(b, carry):
        pt_v[b] = p_v[b].T
        return carry

    lax.fori_loop(0, 3 * FP, transpose, 0)

    def pick(q, first, none):
        return jnp.where((q >= 0) & (q <= 2), first + q, none)

    for i in range(FP):
        for c in range(CP + 2):
            if (c == 0 and i > 2) or (c == CP + 1 and i < FP - 3):
                continue
            r[blk(c), blk(i)] = pt_v[pick(c - agg(i), 3 * i, 3 * FP)]

    ids = []
    for s in range(REP):
        ids.append(rep_s[1, s, dn] - FP)
    for j in range(FP):
        ids.append(j)
    for s in range(REP):
        ids.append(rep_s[0, s, up] + FP)

    load_a.wait()

    def spread(i, carry):
        held = [jnp.where(k < cnt_s[0, i], cols_s[k, i] - e * FP, 1 << 20) for k in range(KA)]
        rows = pl.ds(pl.multiple_of(i * B, B), B)
        for j in range(NJ):
            at = KA * FP
            for k in range(KA):
                at = jnp.where(held[k] == ids[j], i * KA + k, at)
            ad[rows, blk(j)] = a_v[at]
        return carry

    lax.fori_loop(0, FP, spread, 0)

    for c, i in ((0, 0), (CP + 1, FP - 3)):
        for n in range(0, NJ, 6):
            ra[blk(c), blk(n, 6)] = dot(r[blk(c), blk(i, 3)], ad[blk(i, 3), blk(n, 6)]).astype(jnp.bfloat16)

    for j in range(FP):
        for t in range(-1, CP + 1):
            pd[blk(REP + j), blk(t - T0)] = p_v[pick(t - agg(j) + 1, 3 * j, 3 * FP)]

    own = blk(REP, FP)
    for d, c, first, t in ((0, 0, 0, -1), (1, CP + 1, REP + FP, 1)):
        for s in range(REP):
            sendg[d, s] = ra[blk(c), blk(first + s)]
        part = dot(ra[blk(c), own], pd[own, blk(t - T0, 5)]).astype(jnp.bfloat16)
        for n in range(5):
            sendg[d, REP + n] = part[:, n * B : (n + 1) * B]

    pl.when(has_dn & ahead)(start_down)
    for d in (1, 0):
        start(send_g, d)

    mid = blk(1, CP)

    def left(n, carry):
        at = pl.ds(pl.multiple_of(n * 2 * B, 2 * B), 2 * B)
        ra[mid, at] = dot(r[mid, :], ad[:, at]).astype(jnp.bfloat16)
        return carry

    lax.fori_loop(0, NJ // 2, left, 0)

    def emit(t, count, first, panels):
        part = dot(ra[mid, blk(first, panels)], pd[blk(first, panels), blk(t - T0, count)])
        for n in range(count):
            for c in range(CP):
                block = part[c * B : (c + 1) * B, n * B : (n + 1) * B]
                if c in (0, CP - 1):
                    acc[0 if c == 0 else 1, :, blk(t + n - T0)] = block
                else:
                    out[c, t + n - c + 10] = block.astype(jnp.bfloat16)

    last = REP + FP
    arrived(send_p, 0)
    for s in range(REP):
        g = agg_s[rep_s[0, s, up], up] + CP
        for t in range(4, 11):
            pd[blk(last + s), blk(t - T0)] = recvp_up[pick(t - g + 1, 3 * s, 3 * REP)]
    part = dot(ra[blk(0), blk(REP, FP + 1)], pd[blk(REP, FP + 1), blk(4 - T0, 2)]).astype(jnp.bfloat16)
    sendc[0, 0] = part[:, :B]
    sendc[0, 1] = part[:, B:]
    sendc[0, 2] = dot(ra[blk(0), blk(last)], pd[blk(last), blk(6 - T0)]).astype(jnp.bfloat16)
    start(send_c, 0)

    arrived(send_p, 1)
    for s in range(REP):
        g = agg_s[rep_s[1, s, dn], dn] - CP
        for t in range(-6, 1):
            pd[blk(s), blk(t - T0)] = recvp_dn[pick(t - g + 1, 3 * s, 3 * REP)]
    part = dot(ra[blk(CP + 1), blk(REP - 1, FP + 1)], pd[blk(REP - 1, FP + 1), blk(-1 - T0, 2)]).astype(jnp.bfloat16)
    sendc[1, 1] = part[:, :B]
    sendc[1, 2] = part[:, B:]
    sendc[1, 0] = dot(ra[blk(CP + 1), blk(REP - 1)], pd[blk(REP - 1), blk(-2 - T0)]).astype(jnp.bfloat16)
    start(send_c, 1)

    emit(1, 3, REP, FP)
    emit(4, 2, REP, FP + REP)
    emit(6, 5, last, REP)
    emit(-1, 2, 0, REP + FP)
    emit(-6, 5, 0, REP)

    for d in range(2):
        for s in range(REP):
            local = rep_s[d, s, e]
            for t in range(-1, CP + 1):
                pl_own[d, blk(s), blk(t + 1)] = p_v[pick(t - agg(local) + 1, 3 * local, 3 * FP)]

    for c in range(CP):
        for m in range(KC):
            low, high = (3 if c == 0 else CP - 1 - c), (17 if c == CP - 1 else KC - 1 - c)
            if not low <= m <= high:
                out[c, m] = zero

    for d, c, n in ((0, CP - 1, 1), (1, 0, 0)):
        arrived(send_g, d)
        factor = jnp.concatenate([recvg[d, s] for s in range(REP)], axis=1)
        extra = dot(factor, pl_own[n])
        early, late = (1, -2) if d == 1 else (-1, 4)
        held = {}
        for t in range(T0 - 1, T0 + NT + 1):
            m = t - c + 10
            if not 0 <= m < KC:
                continue
            terms = []
            if T0 <= t < T0 + NT:
                terms.append(acc[n, :, blk(t - T0)])
            if -1 <= t <= CP:
                terms.append(extra[:, (t + 1) * B : (t + 2) * B])
            sent = t + CP if d == 1 else t - CP
            if early <= sent < early + 5:
                terms.append(recvg[d, REP + sent - early].astype(jnp.float32))
            total = functools.reduce(jnp.add, terms) if terms else None
            if late <= sent < late + 3:
                if total is not None:
                    acc[n, :, blk(t - T0)] = total
                held[m] = (sent - late, t, total is not None)
            elif terms:
                out[c, m] = total.astype(jnp.bfloat16)
        arrived(send_c, d)
        for m, (at, t, more) in held.items():
            total = recvc[d, at].astype(jnp.float32)
            if more:
                total = total + acc[n, :, blk(t - T0)]
            out[c, m] = total.astype(jnp.bfloat16)

    for copies in (send_p, send_g, send_c):
        for d in range(2):
            pl.when(sends[d])(copies[d].wait_send)


def body(ndev, nsub, a_tiles, a_cols, a_count, p_tiles, aggregate, rep_list):
    bf16 = jnp.bfloat16
    vmem = pltpu.VMEM
    return pl.pallas_call(
        functools.partial(kernel, ndev, nsub),
        out_shape=pltpu.VMEM((CP, KC, B, B), bf16),
        in_specs=[pl.BlockSpec(memory_space=pl.ANY)] * 6,
        out_specs=pl.BlockSpec(memory_space=pltpu.VMEM),
        scratch_shapes=[
            pltpu.SMEM((KA, FP), jnp.int32),
            pltpu.SMEM((1, FP), jnp.int32),
            pltpu.SMEM((FP, ndev), jnp.int32),
            pltpu.SMEM((2, REP, ndev), jnp.int32),
            vmem((3 * FP + 1, B, B), bf16),
            vmem((3 * FP + 1, B, B), bf16),
            vmem((KA * FP + 1, B, B), bf16),
            vmem((FP * B, NJ * B), bf16),
            vmem(((CP + 2) * B, FP * B), bf16),
            vmem(((CP + 2) * B, NJ * B), bf16),
            vmem((NJ * B, NT * B), bf16),
            vmem((2, REP * B, 7 * B), bf16),
            vmem((2, B, NT * B), jnp.float32),
            vmem((2, 3 * REP, B, B), bf16),
            vmem((3 * REP + 1, B, B), bf16),
            vmem((3 * REP + 1, B, B), bf16),
            vmem((2, REP + 5, B, B), bf16),
            vmem((2, REP + 5, B, B), bf16),
            vmem((2, 3, B, B), bf16),
            vmem((2, 3, B, B), bf16),
            pltpu.SemaphoreType.DMA((6,)),
            pltpu.SemaphoreType.DMA((2, 3)),
            pltpu.SemaphoreType.DMA((2, 3)),
            pltpu.SemaphoreType.REGULAR,
        ],
        compiler_params=pltpu.CompilerParams(
            collective_id=0, has_side_effects=True, vmem_limit_bytes=56 << 20
        ),
        name="coarse",
    )(
        a_cols.T,
        a_count.reshape(1, FP),
        aggregate.T,
        rep_list.transpose(1, 2, 0),
        a_tiles.reshape(FP * KA, B, B),
        p_tiles.reshape(FP * 3, B, B),
    )


def solution(mesh):
    in_specs = (
        P(("rows", "sub"), None, None, None),
        P(("rows", "sub"), None),
        P(("rows", "sub")),
        P(("rows", "sub"), None, None, None),
        P(),
        P(),
    )
    out_specs = P(("rows", "sub"), None, None, None)
    run = functools.partial(body, mesh.size, mesh.shape["sub"])
    return jax.shard_map(run, mesh=mesh, in_specs=in_specs, out_specs=out_specs, check_vma=False)
```

```python
import functools

import jax
import jax.numpy as jnp
from jax import lax
from jax.experimental import pallas as pl
from jax.experimental.pallas import tpu as pltpu
from jax.sharding import PartitionSpec as P

B = 128
FP = 10
CP = 5
KA = 8
REP = 4
NJ = FP + 2 * REP
NT = 17
T0 = -6
ROWS_X = 16
KC = 21
MESH = pl.DeviceIdType.MESH


def blk(n, count=1):
    return pl.ds(n * B, count * B)


def dot(x, y):
    return jnp.dot(x, y, preferred_element_type=jnp.float32)


def kernel(
    ndev, nsub,
    cols_h, cnt_h, agg_h, rep_h, a_h, p_h,
    out,
    cols_s, cnt_s, agg_s, rep_s, p_v, pt_v, a_v, ad, r, ra, pd, pl_own, acc,
    sendp, recvp_up, recvp_dn, sendg, recvg, sendc, recvc,
    load_sem, send_sem, recv_sem, ready_sem,
):
    e = lax.axis_index("rows") * nsub + lax.axis_index("sub")
    up = lax.rem(e + 1, ndev)
    dn = lax.rem(e + ndev - 1, ndev)
    peers = ((dn // nsub, lax.rem(dn, nsub)), (up // nsub, lax.rem(up, nsub)))

    has_dn = e > 0
    has_up = e < ndev - 1
    sends, receives = (has_dn, has_up), (has_up, has_dn)

    barrier = pltpu.get_barrier_semaphore()

    @pl.when(has_dn)
    def _():
        pl.semaphore_signal(barrier, inc=1, device_id=peers[0], device_id_type=MESH)

    load_p = pltpu.make_async_copy(p_h, p_v.at[pl.ds(0, 3 * FP)], load_sem.at[0])
    load_p.start()
    meta = [
        pltpu.make_async_copy(src, dst, load_sem.at[2 + n])
        for n, (src, dst) in enumerate(((rep_h, rep_s), (agg_h, agg_s), (cols_h, cols_s), (cnt_h, cnt_s)))
    ]
    for copy in meta:
        copy.start()
    load_a = pltpu.make_async_copy(a_h, a_v.at[pl.ds(0, KA * FP)], load_sem.at[1])

    recvp = (recvp_up, recvp_dn)

    load_a.start()
    zero = jnp.zeros((B, B), jnp.bfloat16)
    p_v[3 * FP] = zero
    pt_v[3 * FP] = zero
    a_v[KA * FP] = zero
    recvp_up[3 * REP] = zero
    recvp_dn[3 * REP] = zero


    @pl.when(has_up)
    def _():
        pl.semaphore_wait(barrier, 1)
        pl.semaphore_signal(ready_sem, inc=1, device_id=peers[1], device_id_type=MESH)

    for copy in meta:
        copy.wait()
    load_p.wait()

    def agg(i):
        return agg_s[i, e]

    for i in range(3):
        low = jnp.where((e == 0) & (agg(i) == 0), 3 * FP, 3 * i)
        p_v[3 * i] = p_v[low]
        k = FP - 1 - i
        high = jnp.where((e == ndev - 1) & (agg(k) == CP - 1), 3 * FP, 3 * k + 2)
        p_v[3 * k + 2] = p_v[high]

    def remote(d, n, src, dst):
        return pltpu.make_async_remote_copy(
            src_ref=src, dst_ref=dst, send_sem=send_sem.at[d, n], recv_sem=recv_sem.at[d, n],
            device_id=peers[d], device_id_type=MESH,
        )

    send_p = [remote(d, 0, sendp.at[d], recvp[d].at[pl.ds(0, 3 * REP)]) for d in range(2)]
    send_g = [remote(d, 1, sendg.at[d], recvg.at[d]) for d in range(2)]
    send_c = [remote(d, 2, sendc.at[d], recvc.at[d]) for d in range(2)]

    def start(copies, d):
        pl.when(sends[d])(copies[d].start)

    def arrived(copies, d):
        pl.when(receives[d])(copies[d].wait_recv)

    for d in (1, 0):
        for s in range(REP):
            local = rep_s[d, s, e]
            for q in range(3):
                sendp[d, 3 * s + q] = p_v[3 * local + q]
        if d == 1:
            start(send_p, d)

    def start_down():
        pl.semaphore_wait(ready_sem, 1)
        send_p[0].start()

    ahead = lax.rem(e, nsub * ROWS_X) == 0
    pl.when(has_dn & jnp.logical_not(ahead))(start_down)

    for d in range(2):
        @pl.when(jnp.logical_not(receives[d]))
        def _():
            recvp[d][...] = jnp.zeros(recvp[d].shape, jnp.bfloat16)
            recvg[d] = jnp.zeros(recvg.shape[1:], jnp.bfloat16)
            recvc[d] = jnp.zeros(recvc.shape[1:], jnp.bfloat16)

    def transpose(b, carry):
        pt_v[b] = p_v[b].T
        return carry

    lax.fori_loop(0, 3 * FP, transpose, 0)

    def pick(q, first, none):
        return jnp.where((q >= 0) & (q <= 2), first + q, none)

    for i in range(FP):
        for c in range(CP + 2):
            if (c == 0 and i > 2) or (c == CP + 1 and i < FP - 3):
                continue
            r[blk(c), blk(i)] = pt_v[pick(c - agg(i), 3 * i, 3 * FP)]

    ids = []
    for s in range(REP):
        ids.append(rep_s[1, s, dn] - FP)
    for j in range(FP):
        ids.append(j)
    for s in range(REP):
        ids.append(rep_s[0, s, up] + FP)

    load_a.wait()

    def spread(i, carry):
        held = [jnp.where(k < cnt_s[0, i], cols_s[k, i] - e * FP, 1 << 20) for k in range(KA)]
        rows = pl.ds(pl.multiple_of(i * B, B), B)
        for j in range(NJ):
            at = KA * FP
            for k in range(KA):
                at = jnp.where(held[k] == ids[j], i * KA + k, at)
            ad[rows, blk(j)] = a_v[at]
        return carry

    lax.fori_loop(0, FP, spread, 0)

    for c, i in ((0, 0), (CP + 1, FP - 3)):
        for n in range(0, NJ, 6):
            ra[blk(c), blk(n, 6)] = dot(r[blk(c), blk(i, 3)], ad[blk(i, 3), blk(n, 6)]).astype(jnp.bfloat16)

    for j in range(FP):
        for t in range(-1, CP + 1):
            pd[blk(REP + j), blk(t - T0)] = p_v[pick(t - agg(j) + 1, 3 * j, 3 * FP)]

    own = blk(REP, FP)
    for d, c, first, t in ((0, 0, 0, -1), (1, CP + 1, REP + FP, 1)):
        for s in range(REP):
            sendg[d, s] = ra[blk(c), blk(first + s)]
        part = dot(ra[blk(c), own], pd[own, blk(t - T0, 5)]).astype(jnp.bfloat16)
        for n in range(5):
            sendg[d, REP + n] = part[:, n * B : (n + 1) * B]

    pl.when(has_dn & ahead)(start_down)
    for d in (1, 0):
        start(send_g, d)

    mid = blk(1, CP)

    def left(n, carry):
        at = pl.ds(pl.multiple_of(n * 2 * B, 2 * B), 2 * B)
        ra[mid, at] = dot(r[mid, :], ad[:, at]).astype(jnp.bfloat16)
        return carry

    lax.fori_loop(0, NJ // 2, left, 0, unroll=3)

    def emit(t, count, first, panels):
        part = dot(ra[mid, blk(first, panels)], pd[blk(first, panels), blk(t - T0, count)])
        for n in range(count):
            for c in range(CP):
                block = part[c * B : (c + 1) * B, n * B : (n + 1) * B]
                if c in (0, CP - 1):
                    acc[0 if c == 0 else 1, :, blk(t + n - T0)] = block
                else:
                    out[c, t + n - c + 10] = block.astype(jnp.bfloat16)

    last = REP + FP
    arrived(send_p, 1)
    for s in range(REP):
        g = agg_s[rep_s[1, s, dn], dn] - CP
        for t in range(-6, 1):
            pd[blk(s), blk(t - T0)] = recvp_dn[pick(t - g + 1, 3 * s, 3 * REP)]
    part = dot(ra[blk(CP + 1), blk(REP - 1, FP + 1)], pd[blk(REP - 1, FP + 1), blk(-1 - T0, 2)]).astype(jnp.bfloat16)
    sendc[1, 1] = part[:, :B]
    sendc[1, 2] = part[:, B:]
    sendc[1, 0] = dot(ra[blk(CP + 1), blk(REP - 1)], pd[blk(REP - 1), blk(-2 - T0)]).astype(jnp.bfloat16)
    start(send_c, 1)

    arrived(send_p, 0)
    for s in range(REP):
        g = agg_s[rep_s[0, s, up], up] + CP
        for t in range(4, 11):
            pd[blk(last + s), blk(t - T0)] = recvp_up[pick(t - g + 1, 3 * s, 3 * REP)]
    part = dot(ra[blk(0), blk(REP, FP + 1)], pd[blk(REP, FP + 1), blk(4 - T0, 2)]).astype(jnp.bfloat16)
    sendc[0, 0] = part[:, :B]
    sendc[0, 1] = part[:, B:]
    sendc[0, 2] = dot(ra[blk(0), blk(last)], pd[blk(last), blk(6 - T0)]).astype(jnp.bfloat16)
    start(send_c, 0)

    emit(1, 3, REP, FP)
    emit(4, 2, REP, FP + REP)
    emit(6, 5, last, REP)
    emit(-1, 2, 0, REP + FP)
    emit(-6, 5, 0, REP)

    for d in range(2):
        for s in range(REP):
            local = rep_s[d, s, e]
            for t in range(-1, CP + 1):
                pl_own[d, blk(s), blk(t + 1)] = p_v[pick(t - agg(local) + 1, 3 * local, 3 * FP)]

    for c in range(CP):
        for m in range(KC):
            low, high = (3 if c == 0 else CP - 1 - c), (17 if c == CP - 1 else KC - 1 - c)
            if not low <= m <= high:
                out[c, m] = zero

    for d, c, n in ((0, CP - 1, 1), (1, 0, 0)):
        arrived(send_g, d)
        factor = jnp.concatenate([recvg[d, s] for s in range(REP)], axis=1)
        extra = dot(factor, pl_own[n])
        early, late = (1, -2) if d == 1 else (-1, 4)
        held = {}
        for t in range(T0 - 1, T0 + NT + 1):
            m = t - c + 10
            if not 0 <= m < KC:
                continue
            terms = []
            if T0 <= t < T0 + NT:
                terms.append(acc[n, :, blk(t - T0)])
            if -1 <= t <= CP:
                terms.append(extra[:, (t + 1) * B : (t + 2) * B])
            sent = t + CP if d == 1 else t - CP
            if early <= sent < early + 5:
                terms.append(recvg[d, REP + sent - early].astype(jnp.float32))
            total = functools.reduce(jnp.add, terms) if terms else None
            if late <= sent < late + 3:
                if total is not None:
                    acc[n, :, blk(t - T0)] = total
                held[m] = (sent - late, t, total is not None)
            elif terms:
                out[c, m] = total.astype(jnp.bfloat16)
        arrived(send_c, d)
        for m, (at, t, more) in held.items():
            total = recvc[d, at].astype(jnp.float32)
            if more:
                total = total + acc[n, :, blk(t - T0)]
            out[c, m] = total.astype(jnp.bfloat16)

    for copies in (send_p, send_g, send_c):
        for d in range(2):
            pl.when(sends[d])(copies[d].wait_send)


def body(ndev, nsub, a_tiles, a_cols, a_count, p_tiles, aggregate, rep_list):
    bf16 = jnp.bfloat16
    vmem = pltpu.VMEM
    return pl.pallas_call(
        functools.partial(kernel, ndev, nsub),
        out_shape=pltpu.VMEM((CP, KC, B, B), bf16),
        in_specs=[pl.BlockSpec(memory_space=pl.ANY)] * 6,
        out_specs=pl.BlockSpec(memory_space=pltpu.VMEM),
        scratch_shapes=[
            pltpu.SMEM((KA, FP), jnp.int32),
            pltpu.SMEM((1, FP), jnp.int32),
            pltpu.SMEM((FP, ndev), jnp.int32),
            pltpu.SMEM((2, REP, ndev), jnp.int32),
            vmem((3 * FP + 1, B, B), bf16),
            vmem((3 * FP + 1, B, B), bf16),
            vmem((KA * FP + 1, B, B), bf16),
            vmem((FP * B, NJ * B), bf16),
            vmem(((CP + 2) * B, FP * B), bf16),
            vmem(((CP + 2) * B, NJ * B), bf16),
            vmem((NJ * B, NT * B), bf16),
            vmem((2, REP * B, 7 * B), bf16),
            vmem((2, B, NT * B), jnp.float32),
            vmem((2, 3 * REP, B, B), bf16),
            vmem((3 * REP + 1, B, B), bf16),
            vmem((3 * REP + 1, B, B), bf16),
            vmem((2, REP + 5, B, B), bf16),
            vmem((2, REP + 5, B, B), bf16),
            vmem((2, 3, B, B), bf16),
            vmem((2, 3, B, B), bf16),
            pltpu.SemaphoreType.DMA((6,)),
            pltpu.SemaphoreType.DMA((2, 3)),
            pltpu.SemaphoreType.DMA((2, 3)),
            pltpu.SemaphoreType.REGULAR,
        ],
        compiler_params=pltpu.CompilerParams(
            collective_id=0, has_side_effects=True, vmem_limit_bytes=56 << 20
        ),
        name="coarse",
    )(
        a_cols.T,
        a_count.reshape(1, FP),
        aggregate.T,
        rep_list.transpose(1, 2, 0),
        a_tiles.reshape(FP * KA, B, B),
        p_tiles.reshape(FP * 3, B, B),
    )


def solution(mesh):
    in_specs = (
        P(("rows", "sub"), None, None, None),
        P(("rows", "sub"), None),
        P(("rows", "sub")),
        P(("rows", "sub"), None, None, None),
        P(),
        P(),
    )
    out_specs = P(("rows", "sub"), None, None, None)
    run = functools.partial(body, mesh.size, mesh.shape["sub"])
    return jax.shard_map(run, mesh=mesh, in_specs=in_specs, out_specs=out_specs, check_vma=False)
```

```python
import functools

import jax
import jax.numpy as jnp
from jax import lax
from jax.experimental import pallas as pl
from jax.experimental.pallas import tpu as pltpu
from jax.sharding import PartitionSpec as P

B = 128
FP = 10
CP = 5
KA = 8
REP = 4
NJ = FP + 2 * REP
NT = 17
T0 = -6
ROWS_X = 16
KC = 21
MESH = pl.DeviceIdType.MESH


def blk(n, count=1):
    return pl.ds(n * B, count * B)


def dot(x, y):
    return jnp.dot(x, y, preferred_element_type=jnp.float32)


def kernel(
    ndev, nsub,
    cols_h, cnt_h, agg_h, rep_h, a_h, p_h,
    out,
    cols_s, cnt_s, agg_s, rep_s, p_v, pt_v, a_v, ad, r, ra, pd, pl_own, acc,
    sendp, recvp_up, recvp_dn, sendg, recvg, sendc, recvc,
    load_sem, send_sem, recv_sem, ready_sem,
):
    e = lax.axis_index("rows") * nsub + lax.axis_index("sub")
    up = lax.rem(e + 1, ndev)
    dn = lax.rem(e + ndev - 1, ndev)
    peers = ((dn // nsub, lax.rem(dn, nsub)), (up // nsub, lax.rem(up, nsub)))

    has_dn = e > 0
    has_up = e < ndev - 1
    sends, receives = (has_dn, has_up), (has_up, has_dn)

    barrier = pltpu.get_barrier_semaphore()

    @pl.when(has_dn)
    def _():
        pl.semaphore_signal(barrier, inc=1, device_id=peers[0], device_id_type=MESH)

    load_p = pltpu.make_async_copy(p_h, p_v.at[pl.ds(0, 3 * FP)], load_sem.at[0])
    load_p.start()
    meta = [
        pltpu.make_async_copy(src, dst, load_sem.at[2 + n])
        for n, (src, dst) in enumerate(((rep_h, rep_s), (agg_h, agg_s), (cols_h, cols_s), (cnt_h, cnt_s)))
    ]
    for copy in meta:
        copy.start()
    load_a = pltpu.make_async_copy(a_h, a_v.at[pl.ds(0, KA * FP)], load_sem.at[1])

    recvp = (recvp_up, recvp_dn)

    load_a.start()
    zero = jnp.zeros((B, B), jnp.bfloat16)
    p_v[3 * FP] = zero
    pt_v[3 * FP] = zero
    a_v[KA * FP] = zero
    recvp_up[3 * REP] = zero
    recvp_dn[3 * REP] = zero


    @pl.when(has_up)
    def _():
        pl.semaphore_wait(barrier, 1)
        pl.semaphore_signal(ready_sem, inc=1, device_id=peers[1], device_id_type=MESH)

    for copy in meta:
        copy.wait()
    load_p.wait()

    def agg(i):
        return agg_s[i, e]

    for i in range(3):
        low = jnp.where((e == 0) & (agg(i) == 0), 3 * FP, 3 * i)
        p_v[3 * i] = p_v[low]
        k = FP - 1 - i
        high = jnp.where((e == ndev - 1) & (agg(k) == CP - 1), 3 * FP, 3 * k + 2)
        p_v[3 * k + 2] = p_v[high]

    def remote(d, n, src, dst):
        return pltpu.make_async_remote_copy(
            src_ref=src, dst_ref=dst, send_sem=send_sem.at[d, n], recv_sem=recv_sem.at[d, n],
            device_id=peers[d], device_id_type=MESH,
        )

    send_p = [remote(d, 0, sendp.at[d], recvp[d].at[pl.ds(0, 3 * REP)]) for d in range(2)]
    send_g = [remote(d, 1, sendg.at[d], recvg.at[d]) for d in range(2)]
    send_c = [remote(d, 2, sendc.at[d], recvc.at[d]) for d in range(2)]

    def start(copies, d):
        pl.when(sends[d])(copies[d].start)

    def arrived(copies, d):
        pl.when(receives[d])(copies[d].wait_recv)

    for d in (1, 0):
        for s in range(REP):
            local = rep_s[d, s, e]
            for q in range(3):
                sendp[d, 3 * s + q] = p_v[3 * local + q]
        if d == 1:
            start(send_p, d)

    def start_down():
        pl.semaphore_wait(ready_sem, 1)
        send_p[0].start()

    ahead = lax.rem(e, nsub * ROWS_X) == 0
    pl.when(has_dn & jnp.logical_not(ahead))(start_down)

    for d in range(2):
        @pl.when(jnp.logical_not(receives[d]))
        def _():
            recvp[d][...] = jnp.zeros(recvp[d].shape, jnp.bfloat16)
            recvg[d] = jnp.zeros(recvg.shape[1:], jnp.bfloat16)
            recvc[d] = jnp.zeros(recvc.shape[1:], jnp.bfloat16)

    def transpose(b, carry):
        pt_v[b] = p_v[b].T
        return carry

    lax.fori_loop(0, 3 * FP, transpose, 0)

    def pick(q, first, none):
        return jnp.where((q >= 0) & (q <= 2), first + q, none)

    for i in range(FP):
        for c in range(CP + 2):
            if (c == 0 and i > 2) or (c == CP + 1 and i < FP - 3):
                continue
            r[blk(c), blk(i)] = pt_v[pick(c - agg(i), 3 * i, 3 * FP)]

    ids = []
    for s in range(REP):
        ids.append(rep_s[1, s, dn] - FP)
    for j in range(FP):
        ids.append(j)
    for s in range(REP):
        ids.append(rep_s[0, s, up] + FP)

    load_a.wait()

    def spread(i, carry):
        held = [jnp.where(k < cnt_s[0, i], cols_s[k, i] - e * FP, 1 << 20) for k in range(KA)]
        rows = pl.ds(pl.multiple_of(i * B, B), B)
        for j in range(NJ):
            at = KA * FP
            for k in range(KA):
                at = jnp.where(held[k] == ids[j], i * KA + k, at)
            ad[rows, blk(j)] = a_v[at]
        return carry

    lax.fori_loop(0, FP, spread, 0)

    for c, i in ((0, 0), (CP + 1, FP - 3)):
        for n in range(0, NJ, 6):
            ra[blk(c), blk(n, 6)] = dot(r[blk(c), blk(i, 3)], ad[blk(i, 3), blk(n, 6)]).astype(jnp.bfloat16)

    for j in range(FP):
        for t in range(-1, CP + 1):
            pd[blk(REP + j), blk(t - T0)] = p_v[pick(t - agg(j) + 1, 3 * j, 3 * FP)]

    own = blk(REP, FP)
    for d, c, first, t in ((0, 0, 0, -1), (1, CP + 1, REP + FP, 1)):
        for s in range(REP):
            sendg[d, s] = ra[blk(c), blk(first + s)]
        part = dot(ra[blk(c), own], pd[own, blk(t - T0, 5)]).astype(jnp.bfloat16)
        for n in range(5):
            sendg[d, REP + n] = part[:, n * B : (n + 1) * B]

    pl.when(has_dn & ahead)(start_down)

    mid = blk(1, CP)

    def left(n, carry):
        at = pl.ds(pl.multiple_of(n * 2 * B, 2 * B), 2 * B)
        ra[mid, at] = dot(r[mid, :], ad[:, at]).astype(jnp.bfloat16)
        return carry

    lax.fori_loop(0, 3, left, 0, unroll=3)
    for d in (1, 0):
        start(send_g, d)
    lax.fori_loop(3, NJ // 2, left, 0, unroll=3)

    def emit(t, count, first, panels):
        part = dot(ra[mid, blk(first, panels)], pd[blk(first, panels), blk(t - T0, count)])
        for n in range(count):
            for c in range(CP):
                block = part[c * B : (c + 1) * B, n * B : (n + 1) * B]
                if c in (0, CP - 1):
                    acc[0 if c == 0 else 1, :, blk(t + n - T0)] = block
                else:
                    out[c, t + n - c + 10] = block.astype(jnp.bfloat16)

    last = REP + FP
    arrived(send_p, 1)
    for s in range(REP):
        g = agg_s[rep_s[1, s, dn], dn] - CP
        for t in range(-6, 1):
            pd[blk(s), blk(t - T0)] = recvp_dn[pick(t - g + 1, 3 * s, 3 * REP)]
    part = dot(ra[blk(CP + 1), blk(REP - 1, FP + 1)], pd[blk(REP - 1, FP + 1), blk(-1 - T0, 2)]).astype(jnp.bfloat16)
    sendc[1, 1] = part[:, :B]
    sendc[1, 2] = part[:, B:]
    sendc[1, 0] = dot(ra[blk(CP + 1), blk(REP - 1)], pd[blk(REP - 1), blk(-2 - T0)]).astype(jnp.bfloat16)
    start(send_c, 1)

    arrived(send_p, 0)
    for s in range(REP):
        g = agg_s[rep_s[0, s, up], up] + CP
        for t in range(4, 11):
            pd[blk(last + s), blk(t - T0)] = recvp_up[pick(t - g + 1, 3 * s, 3 * REP)]
    part = dot(ra[blk(0), blk(REP, FP + 1)], pd[blk(REP, FP + 1), blk(4 - T0, 2)]).astype(jnp.bfloat16)
    sendc[0, 0] = part[:, :B]
    sendc[0, 1] = part[:, B:]
    sendc[0, 2] = dot(ra[blk(0), blk(last)], pd[blk(last), blk(6 - T0)]).astype(jnp.bfloat16)
    start(send_c, 0)

    emit(1, 3, REP, FP)
    emit(4, 2, REP, FP + REP)
    emit(6, 5, last, REP)
    emit(-1, 2, 0, REP + FP)
    emit(-6, 5, 0, REP)

    for d in range(2):
        for s in range(REP):
            local = rep_s[d, s, e]
            for t in range(-1, CP + 1):
                pl_own[d, blk(s), blk(t + 1)] = p_v[pick(t - agg(local) + 1, 3 * local, 3 * FP)]

    for c in range(CP):
        for m in range(KC):
            low, high = (3 if c == 0 else CP - 1 - c), (17 if c == CP - 1 else KC - 1 - c)
            if not low <= m <= high:
                out[c, m] = zero

    for d, c, n in ((0, CP - 1, 1), (1, 0, 0)):
        arrived(send_g, d)
        factor = jnp.concatenate([recvg[d, s] for s in range(REP)], axis=1)
        extra = dot(factor, pl_own[n])
        early, late = (1, -2) if d == 1 else (-1, 4)
        held = {}
        for t in range(T0 - 1, T0 + NT + 1):
            m = t - c + 10
            if not 0 <= m < KC:
                continue
            terms = []
            if T0 <= t < T0 + NT:
                terms.append(acc[n, :, blk(t - T0)])
            if -1 <= t <= CP:
                terms.append(extra[:, (t + 1) * B : (t + 2) * B])
            sent = t + CP if d == 1 else t - CP
            if early <= sent < early + 5:
                terms.append(recvg[d, REP + sent - early].astype(jnp.float32))
            total = functools.reduce(jnp.add, terms) if terms else None
            if late <= sent < late + 3:
                if total is not None:
                    acc[n, :, blk(t - T0)] = total
                held[m] = (sent - late, t, total is not None)
            elif terms:
                out[c, m] = total.astype(jnp.bfloat16)
        arrived(send_c, d)
        for m, (at, t, more) in held.items():
            total = recvc[d, at].astype(jnp.float32)
            if more:
                total = total + acc[n, :, blk(t - T0)]
            out[c, m] = total.astype(jnp.bfloat16)

    for copies in (send_p, send_g, send_c):
        for d in range(2):
            pl.when(sends[d])(copies[d].wait_send)


def body(ndev, nsub, a_tiles, a_cols, a_count, p_tiles, aggregate, rep_list):
    bf16 = jnp.bfloat16
    vmem = pltpu.VMEM
    return pl.pallas_call(
        functools.partial(kernel, ndev, nsub),
        out_shape=pltpu.VMEM((CP, KC, B, B), bf16),
        in_specs=[pl.BlockSpec(memory_space=pl.ANY)] * 6,
        out_specs=pl.BlockSpec(memory_space=pltpu.VMEM),
        scratch_shapes=[
            pltpu.SMEM((KA, FP), jnp.int32),
            pltpu.SMEM((1, FP), jnp.int32),
            pltpu.SMEM((FP, ndev), jnp.int32),
            pltpu.SMEM((2, REP, ndev), jnp.int32),
            vmem((3 * FP + 1, B, B), bf16),
            vmem((3 * FP + 1, B, B), bf16),
            vmem((KA * FP + 1, B, B), bf16),
            vmem((FP * B, NJ * B), bf16),
            vmem(((CP + 2) * B, FP * B), bf16),
            vmem(((CP + 2) * B, NJ * B), bf16),
            vmem((NJ * B, NT * B), bf16),
            vmem((2, REP * B, 7 * B), bf16),
            vmem((2, B, NT * B), jnp.float32),
            vmem((2, 3 * REP, B, B), bf16),
            vmem((3 * REP + 1, B, B), bf16),
            vmem((3 * REP + 1, B, B), bf16),
            vmem((2, REP + 5, B, B), bf16),
            vmem((2, REP + 5, B, B), bf16),
            vmem((2, 3, B, B), bf16),
            vmem((2, 3, B, B), bf16),
            pltpu.SemaphoreType.DMA((6,)),
            pltpu.SemaphoreType.DMA((2, 3)),
            pltpu.SemaphoreType.DMA((2, 3)),
            pltpu.SemaphoreType.REGULAR,
        ],
        compiler_params=pltpu.CompilerParams(
            collective_id=0, has_side_effects=True, vmem_limit_bytes=56 << 20
        ),
        name="coarse",
    )(
        a_cols.T,
        a_count.reshape(1, FP),
        aggregate.T,
        rep_list.transpose(1, 2, 0),
        a_tiles.reshape(FP * KA, B, B),
        p_tiles.reshape(FP * 3, B, B),
    )


def solution(mesh):
    in_specs = (
        P(("rows", "sub"), None, None, None),
        P(("rows", "sub"), None),
        P(("rows", "sub")),
        P(("rows", "sub"), None, None, None),
        P(),
        P(),
    )
    out_specs = P(("rows", "sub"), None, None, None)
    run = functools.partial(body, mesh.size, mesh.shape["sub"])
    return jax.shard_map(run, mesh=mesh, in_specs=in_specs, out_specs=out_specs, check_vma=False)
```
